32 devices in a mesh: gx: 4 (over x, core), gy: 2 (over y), gz: 4 (over z).
Axes of the slice: x: 2, y: 2, z: 4, core: 2. Of those that a mesh axis runs over, the one named last changes fastest.
Arguments:
- density: float32 [128, 512, 512], P('gz', 'gy', 'gx'), may hold values from 0.05 to 0.95
- design_mask: int32 [128, 512, 512], P('gz', 'gy', 'gx'), may hold values 0 or 1
- velocity: bfloat16 [3, 128, 512, 512], P(None, 'gz', 'gy', 'gx'), may hold values from -6 to 6
- adjoint_source: bfloat16 [3, 128, 512, 512], P(None, 'gz', 'gy', 'gx'), may hold values from -6 to 6
- adjoint_start: float32 [3, 128, 512, 512], P(None, 'gz', 'gy', 'gx'), may hold values from -4 to 4
Outputs:
- density_next: float32 [128, 512, 512], P('gz', 'gy', 'gx')
- adjoint: float32 [3, 128, 512, 512], P(None, 'gz', 'gy', 'gx')
The draws below stay inside these ranges and needn't reach their ends.
All inputs are finite; a program needn't handle non-finite values. No bound on the sum of `design_mask` on one device may be relied on, other than what follows from the above.
Results may differ from the reference program's by a relative error of at most 0.0003.
Values sent between devices are 32-bit elements; how exact they have to be, the bound alone decides.
A program may use at most 256 MiB of HBM per device.

```python
import jax
import jax.numpy as jnp
from jax import lax

NX = 512
NY = 512
RADIUS = 32
RADIUS_Z = 16
SWEEPS = 2
NZ = 128


def draw_velocity(key, part):
    key = jax.random.fold_in(key, 11)
    values = jax.random.truncated_normal(key, -6.0, 6.0, (3, NZ, NY, NX), jnp.float32)
    return values.astype(jnp.bfloat16)


def draw_adjoint_source(key, part):
    key = jax.random.fold_in(key, 12)
    values = jax.random.truncated_normal(key, -6.0, 6.0, (3, NZ, NY, NX), jnp.float32)
    return values.astype(jnp.bfloat16)


def draw_adjoint_start(key, part):
    key = jax.random.fold_in(key, 13)
    values = 0.5 * jax.random.truncated_normal(key, -8.0, 8.0, (3, NZ, NY, NX), jnp.float32)
    return values.astype(jnp.float32)


def with_ends(array, own_key, low, largest):
    longest = array.shape.index(max(array.shape))
    spots = []
    for shift in (0, 1):
        where = [jax.random.randint(jax.random.fold_in(own_key, axis), (), 0, length) for axis, length in enumerate(array.shape)]
        where[longest] = (where[longest] + shift) % array.shape[longest]
        spots.append(tuple(where))
    return array.at[spots[0]].set(low).at[spots[1]].set(largest)


def steps_of(stream_key, shape, split, least, high):
    factor_of = 1.0
    for axis_at, blocks in split:
        steps = jax.random.uniform(jax.random.fold_in(jax.random.fold_in(stream_key, 6), axis_at), (blocks,), jnp.float32, least / len(split), high / len(split))
        factor_of = factor_of * jnp.repeat(jnp.exp(steps), shape[axis_at] // blocks).reshape((-1,) + (1,) * (len(shape) - 1 - axis_at))
    return factor_of


def setup_inputs(seed: int = 0) -> dict:
    key_of = jax.random.split(jax.random.key(seed), 6)
    return {
        "density": jnp.clip(0.05 + 0.9 * jax.random.uniform(key_of[0], (NZ, NY, NX), jnp.float32) ** steps_of(key_of[0], (NZ, NY, NX), ((0, 4), (1, 2), (2, 4)), -0.2, 0.2), 0.05, 0.95),
        "design_mask": with_ends((jax.random.randint(key_of[1], (NZ, NY, NX), 0, 8) < 1).astype(jnp.int32), jax.random.fold_in(key_of[1], 1), 0, 1),
        "velocity": draw_velocity(jax.random.fold_in(key_of[5], 71), 0),
        "adjoint_source": draw_adjoint_source(jax.random.fold_in(key_of[5], 71), 0),
        "adjoint_start": draw_adjoint_start(jax.random.fold_in(key_of[5], 71), 0),
    }


OMEGA = 0.8
ALPHA_MAX = 12.0
MOVE_STEP = 8.0

def cone_weights():
    rows = jnp.arange(NY, dtype=jnp.int32)
    cols = jnp.arange(NX, dtype=jnp.int32)
    row_dist = jnp.minimum(rows, NY - rows).astype(jnp.float32)
    col_dist = jnp.minimum(cols, NX - cols).astype(jnp.float32)
    radial = jnp.sqrt(row_dist[:, None] ** 2 + col_dist[None, :] ** 2)
    weights = jnp.maximum(jnp.float32(RADIUS) - radial, jnp.float32(0.0))
    return weights / jnp.sum(weights)

def reference(density, design_mask, velocity, adjoint_source, adjoint_start):
    resist = ALPHA_MAX * (1.0 - density) / (1.0 + density)
    diagonal = 6.0 + resist
    source = adjoint_source.astype(jnp.float32)
    adjoint = adjoint_start
    for sweep_index in range(SWEEPS):
        beside = jnp.roll(adjoint, -1, 1) + jnp.roll(adjoint, 1, 1)
        beside = beside + jnp.roll(adjoint, -1, 2) + jnp.roll(adjoint, 1, 2)
        beside = beside + jnp.roll(adjoint, -1, 3) + jnp.roll(adjoint, 1, 3)
        adjoint = adjoint + OMEGA * (source - (diagonal * adjoint - beside)) / diagonal
    slope = -2.0 * ALPHA_MAX / (1.0 + density) ** 2
    sensitivity = slope * lax.optimization_barrier(jnp.sum(velocity.astype(jnp.float32) * adjoint, axis=0))
    norm_z = jnp.float32((RADIUS_Z + 1) ** 2)
    smoothed = jnp.zeros_like(sensitivity)
    for offset in range(-RADIUS_Z, RADIUS_Z + 1):
        weight = jnp.float32(RADIUS_Z + 1 - abs(offset)) / norm_z
        smoothed = smoothed + weight * jnp.roll(sensitivity, -offset, 0)
    spectrum = jnp.fft.fft2(cone_weights()).real
    filtered = jnp.fft.ifft2(jnp.fft.fft2(smoothed, axes=(1, 2)) * spectrum[None], axes=(1, 2)).real
    filtered = filtered.astype(density.dtype)
    updated = jnp.clip(density - MOVE_STEP * filtered, 0.0, 1.0)
    density_next = jnp.where(design_mask == 1, jnp.zeros_like(updated), updated)
    return (density_next, adjoint)
```

```python
import functools
import math

import jax
import jax.numpy as jnp
import ml_dtypes
import numpy as np
from jax import lax
from jax.experimental import pallas as pl
from jax.experimental.pallas import tpu as pltpu
from jax.sharding import PartitionSpec as P

NX = 512
NY = 512
RADIUS = 32
RADIUS_Z = 16
OMEGA = 0.8
ALPHA_MAX = 12.0
MOVE_STEP = 8.0
GROUP = 4
LANES = 128
VMEM = 48 * 2**20


def params():
    return pltpu.CompilerParams(
        vmem_limit_bytes=VMEM, dimension_semantics=("arbitrary",)
    )


def cost(flops, size):
    return pl.CostEstimate(flops=int(flops), bytes_accessed=int(size), transcendentals=0)


def to_next(array, axis):
    count = lax.axis_size(axis)
    return lax.ppermute(array, axis, [(i, (i + 1) % count) for i in range(count)])


def to_prev(array, axis):
    count = lax.axis_size(axis)
    return lax.ppermute(array, axis, [((i + 1) % count, i) for i in range(count)])


def pack_faces(plane, lane, column, xlo, xhi, ylo, yhi):
    height = plane.shape[0]
    here = lane == column
    xlo[...] = jnp.where(here, pltpu.roll(plane, column, 1), xlo[...])
    xhi[...] = jnp.where(here, pltpu.roll(plane, column + 1, 1), xhi[...])
    ylo[pl.ds(column, 1), :] = plane[0:1]
    yhi[pl.ds(column, 1), :] = plane[height - 1 : height]


def faces_kernel(depth, adj, xlo, xhi, ylo, yhi):
    step = pl.program_id(0)

    @pl.when(step == 0)
    def _():
        for ref in (xlo, xhi, ylo, yhi):
            ref[...] = jnp.zeros_like(ref)

    lane = lax.broadcasted_iota(jnp.int32, xlo.shape, 1)
    for j in range(GROUP):
        for c in range(3):
            pack_faces(
                adj[c, j], lane, c * depth + step * GROUP + j, xlo, xhi, ylo, yhi
            )


def face_shapes(depth, height):
    return [jax.ShapeDtypeStruct((height, LANES), jnp.float32)] * 2 + [
        jax.ShapeDtypeStruct((3 * depth, LANES), jnp.float32)
    ] * 2


def whole_spec(shape):
    return pl.BlockSpec(shape, lambda i: (0,) * len(shape))


def faces_of(adjoint):
    _, depth, height, width = adjoint.shape
    shapes = face_shapes(depth, height)
    return pl.pallas_call(
        functools.partial(faces_kernel, depth),
        grid=(depth // GROUP,),
        in_specs=[pl.BlockSpec((3, GROUP, height, width), lambda i: (0, i, 0, 0))],
        out_specs=[whole_spec(s.shape) for s in shapes],
        out_shape=shapes,
        compiler_params=params(),
        cost_estimate=cost(10 * adjoint.size, 4 * adjoint.size),
        name="faces",
    )(adjoint)


def sweep_kernel(conf, *refs):
    depth, first, stride, use_lo, use_hi, faces, fresh, sens = conf
    refs = list(refs)
    adj, prev, follow, source, density, xleft, xright, yabove, ybelow = refs[:9]
    refs = refs[9:]
    zlo = refs.pop(0) if use_lo else None
    zhi = refs.pop(0) if use_hi else None
    velocity = refs.pop(0) if sens else None
    if faces and not fresh:
        held = refs[:4]
        refs = refs[4:]
    aliased = conf.aliased
    refs = refs[aliased:]
    out = refs.pop(0)
    if faces:
        packs = refs[:4]
        refs = refs[4:]
    if sens:
        sens_out, pack_lo, pack_hi = refs
    step = pl.program_id(0)
    block = first + stride * step
    height, width = out.shape[2:]
    if faces:

        @pl.when(step == 0)
        def _():
            for at in range(4):
                if fresh:
                    packs[at][...] = jnp.zeros_like(packs[at])
                else:
                    packs[at][...] = held[at][...]

    lane = lax.broadcasted_iota(jnp.int32, (height, width), 1)
    row = lax.broadcasted_iota(jnp.int32, (height, width), 0)
    last_block = depth // GROUP - 1
    for j in range(GROUP):
        dens = density[j]
        weight = OMEGA * (1.0 + dens) / (18.0 - 6.0 * dens)
        total = None
        for c in range(3):
            column = c * depth + block * GROUP + j
            plane = adj[c, j]
            if j > 0:
                below = adj[c, j - 1]
            else:
                below = prev[c, 0]
                if use_lo:
                    below = jnp.where(block == 0, zlo[c], below)
            if j < GROUP - 1:
                above = adj[c, j + 1]
            else:
                above = follow[c, 0]
                if use_hi:
                    above = jnp.where(block == last_block, zhi[c], above)
            beside = above + below
            beside += jnp.where(
                row == 0, yabove[pl.ds(column, 1), :], pltpu.roll(plane, 1, 0)
            )
            beside += jnp.where(
                row == height - 1,
                ybelow[pl.ds(column, 1), :],
                pltpu.roll(plane, height - 1, 0),
            )
            beside += jnp.where(
                lane == 0,
                pltpu.roll(xleft[...], (LANES - column) % LANES, 1),
                pltpu.roll(plane, 1, 1),
            )
            beside += jnp.where(
                lane == width - 1,
                pltpu.roll(xright[...], LANES - 1 - column, 1),
                pltpu.roll(plane, width - 1, 1),
            )
            relaxed = (1.0 - OMEGA) * plane + weight * (
                source[c, j].astype(jnp.float32) + beside
            )
            out[c, j] = relaxed
            if faces:
                pack_faces(relaxed, lane, column, *packs)
            if sens:
                part = velocity[c, j].astype(jnp.float32) * relaxed
                total = part if total is None else total + part
        if sens:
            near = 1.0 / (1.0 + dens)
            value = (-2.0 * ALPHA_MAX) * near * near * total
            sens_out[j] = value
            turned = pltpu.roll(value, RADIUS * (j + 1) % LANES, 1)
            group = lane // RADIUS
            low = jnp.where(group == (j + 1) % GROUP, turned, 0.0)
            high = jnp.where(group == j, turned, 0.0)
            if j == 0:
                pack_lo[0] = low
                pack_hi[0] = high
            else:
                pack_lo[0] += low
                pack_hi[0] += high


class Conf(tuple):
    aliased = 0


def sweep(
    adjoint,
    source,
    density,
    arrived,
    first,
    count,
    stride=1,
    zlo=None,
    zhi=None,
    faces=False,
    held=None,
    velocity=None,
    sens_base=0,
    onto=(),
):
    _, depth, height, width = adjoint.shape
    sens = velocity is not None
    conf = Conf(
        (depth, first, stride, zlo is not None, zhi is not None, faces, held is None, sens)
    )
    conf.aliased = len(onto)

    def at(i):
        return first + stride * i

    block = pl.BlockSpec((3, GROUP, height, width), lambda i: (0, at(i), 0, 0))
    plane_shape = (3, 1, height, width)
    operands = [adjoint, adjoint, adjoint, source, density, *arrived]
    in_specs = [
        block,
        pl.BlockSpec(plane_shape, lambda i: (0, jnp.maximum(at(i) * GROUP - 1, 0), 0, 0)),
        pl.BlockSpec(
            plane_shape, lambda i: (0, jnp.minimum(at(i) * GROUP + GROUP, depth - 1), 0, 0)
        ),
        block,
        pl.BlockSpec((GROUP, height, width), lambda i: (at(i), 0, 0)),
    ]
    in_specs += [whole_spec(a.shape) for a in arrived]
    for face in (zlo, zhi):
        if face is not None:
            operands.append(face)
            in_specs.append(whole_spec(face.shape))
    if sens:
        operands.append(velocity)
        in_specs.append(block)
    if held is not None:
        operands += list(held)
        in_specs += [whole_spec(a.shape) for a in held]
    aliases = {}
    for index, array in onto:
        aliases[len(operands)] = index
        operands.append(array)
        in_specs.append(pl.BlockSpec(memory_space=pl.ANY))
    out_specs = [block]
    out_shape = [jax.ShapeDtypeStruct(adjoint.shape, jnp.float32)]
    if faces:
        shapes = face_shapes(depth, height)
        out_shape += shapes
        out_specs += [whole_spec(s.shape) for s in shapes]
    if sens:
        half = depth // 2
        out_shape += [jax.ShapeDtypeStruct((half, height, width), jnp.float32)] + [
            jax.ShapeDtypeStruct((half // GROUP, height, LANES), jnp.float32)
        ] * 2
        out_specs += [
            pl.BlockSpec((GROUP, height, width), lambda i: (at(i) - sens_base, 0, 0))
        ] + [pl.BlockSpec((1, height, LANES), lambda i: (at(i) - sens_base, 0, 0))] * 2
    cells = 3 * GROUP * count * height * width
    return pl.pallas_call(
        functools.partial(sweep_kernel, conf),
        grid=(count,),
        in_specs=in_specs,
        out_specs=out_specs,
        out_shape=out_shape,
        input_output_aliases=aliases,
        compiler_params=params(),
        cost_estimate=cost(40 * cells, 14 * cells),
        name="sweep",
    )(*operands)


def parts_of(table):
    high = table.astype(ml_dtypes.bfloat16)
    low = (table - high.astype(np.float64)).astype(ml_dtypes.bfloat16)
    return jnp.asarray(high), jnp.asarray(low)


def real_dft(length):
    half = length // 2
    waves = np.concatenate([np.arange(half + 1), np.arange(1, half)])
    phase = 2.0 * math.pi / length * (waves[:, None] * np.arange(length)[None, :] % length)
    table = np.where(np.arange(length)[:, None] <= half, np.cos(phase), np.sin(phase))
    scale = np.full((length, 1), math.sqrt(2.0 / length))
    scale[0] = scale[half] = math.sqrt(1.0 / length)
    return table * scale, waves


def cone_tables(height, width):
    long_x = -(-(width + 2 * RADIUS) // LANES) * LANES
    long_y = height + 2 * RADIUS
    basis_x, waves_x = real_dft(long_x)
    basis_y, waves_y = real_dft(long_y)
    reach = np.arange(-RADIUS, RADIUS + 1)
    cone = np.maximum(0.0, RADIUS - np.sqrt(reach[:, None] ** 2.0 + reach[None, :] ** 2.0))
    cone = cone / np.sum(cone)
    cos_y = np.cos(2.0 * math.pi / long_y * waves_y[:, None] * reach[None, :])
    cos_x = np.cos(2.0 * math.pi / long_x * waves_x[:, None] * reach[None, :])
    spectrum = (cos_y @ cone @ cos_x.T).astype(np.float32)
    into_x = np.zeros((GROUP, width + LANES, long_x))
    for j in range(GROUP):
        into_x[j, :width] = basis_x[:, RADIUS : RADIUS + width].T
        left = width + RADIUS * j
        into_x[j, left : left + RADIUS] = basis_x[:, :RADIUS].T
        right = width + RADIUS * ((j + 1) % GROUP)
        into_x[j, right : right + RADIUS] = basis_x[:, RADIUS + width : 2 * RADIUS + width].T
    tables = [
        *parts_of(into_x),
        *parts_of(basis_y),
        *parts_of(basis_y[:, RADIUS : RADIUS + height].T),
        *parts_of(basis_x[:, RADIUS : RADIUS + width]),
        jnp.asarray(spectrum),
    ]
    return tables


def split(value):
    high = value.astype(jnp.bfloat16)
    return high, (value - high.astype(jnp.float32)).astype(jnp.bfloat16)


def product(left, right):
    dot = functools.partial(jnp.dot, preferred_element_type=jnp.float32)
    return dot(left[0], right[0]) + (dot(left[0], right[1]) + dot(left[1], right[0]))


def cone_kernel(
    own, left, right,
    above, above_left, above_right,
    below, below_left, below_right,
    into_high, into_low, y_high, y_low, yback_high, yback_low, xback_high, xback_low,
    spectrum, out,
):
    for j in range(GROUP):

        def wide(mid, lhs, rhs):
            group = lax.broadcasted_iota(jnp.int32, lhs.shape, 1) // RADIUS
            return jnp.concatenate([mid, jnp.where(group == j, lhs, rhs)], axis=1)

        cells = jnp.concatenate(
            [
                wide(above[j], above_left[0], above_right[0]),
                wide(own[j], left[0], right[0]),
                wide(below[j], below_left[0], below_right[0]),
            ],
            axis=0,
        )
        waves = product(split(cells), (into_high[j], into_low[j]))
        waves = product((y_high[...], y_low[...]), split(waves)) * spectrum[...]
        rows = product((yback_high[...], yback_low[...]), split(waves))
        out[j] = product(split(rows), (xback_high[...], xback_low[...]))


def cone_filter(sens, pack_lo, pack_hi, tables):
    planes, height, width = sens.shape
    steps = planes // GROUP
    left = to_next(pack_hi, "gx")
    right = to_prev(pack_lo, "gx")
    strips = [sens, left, right]
    above = to_next(
        jnp.concatenate([s[:, height - RADIUS :] for s in strips], axis=0), "gy"
    )
    below = to_prev(jnp.concatenate([s[:, :RADIUS] for s in strips], axis=0), "gy")
    packed = pl.BlockSpec((1, height, LANES), lambda i: (i, 0, 0))
    strip_specs = [
        pl.BlockSpec((GROUP, RADIUS, width), lambda i: (i, 0, 0)),
        pl.BlockSpec((1, RADIUS, LANES), lambda i: (planes + i, 0, 0)),
        pl.BlockSpec((1, RADIUS, LANES), lambda i: (planes + steps + i, 0, 0)),
    ]
    block = pl.BlockSpec((GROUP, height, width), lambda i: (i, 0, 0))
    long_y = height + 2 * RADIUS
    return pl.pallas_call(
        cone_kernel,
        grid=(steps,),
        in_specs=[block, packed, packed]
        + strip_specs * 2
        + [whole_spec(t.shape) for t in tables],
        out_specs=block,
        out_shape=jax.ShapeDtypeStruct(sens.shape, jnp.float32),
        compiler_params=params(),
        cost_estimate=cost(planes * 12 * long_y * 256 * (long_y + 256), 16 * sens.size),
        name="cone",
    )(sens, left, right, above, above, above, below, below, below, *tables)


def step_kernel(first, second, third, density, mask, *rest):
    out = rest[-1]
    planes, rows = out.shape[:2]
    length = RADIUS_Z + 1
    parts = (first, second, third)
    for start in range(0, rows, 8):
        at = slice(start, start + 8)

        def cell(z):
            return parts[z // planes][z % planes, at]

        box = cell(0)
        for z in range(1, length):
            box = box + cell(z)
        boxes = [box]
        for z in range(1, 2 * planes):
            box = box + (cell(z + length - 1) - cell(z - 1))
            boxes.append(box)
        tent = boxes[0]
        for z in range(1, length):
            tent = tent + boxes[z]
        for z in range(planes):
            if z > 0:
                tent = tent + (boxes[z + length - 1] - boxes[z - 1])
            moved = density[z, at] - (MOVE_STEP / float(length * length)) * tent
            moved = jnp.minimum(jnp.maximum(moved, 0.0), 1.0)
            out[z, at] = jnp.where(mask[z, at] == 1, 0.0, moved)


def density_step(first, second, third, density, mask, half, onto=None):
    planes, height, width = first.shape
    rows = 32
    block = pl.BlockSpec((planes, rows, width), lambda i: (0, i, 0))
    placed = pl.BlockSpec((planes, rows, width), lambda i: (half, i, 0))
    operands = [first, second, third, density, mask]
    in_specs = [block] * 3 + [placed] * 2
    aliases = {}
    if onto is not None:
        aliases[len(operands)] = 0
        operands.append(onto)
        in_specs.append(pl.BlockSpec(memory_space=pl.ANY))
    return pl.pallas_call(
        step_kernel,
        grid=(height // rows,),
        in_specs=in_specs,
        out_specs=placed,
        out_shape=jax.ShapeDtypeStruct(density.shape, jnp.float32),
        input_output_aliases=aliases,
        compiler_params=params(),
        cost_estimate=cost(12 * first.size, 24 * first.size),
        name="step",
    )(*operands)


def exchange(faces):
    xlo, xhi, ylo, yhi = faces
    return (
        to_next(xhi, "gx"),
        to_prev(xlo, "gx"),
        to_next(yhi, "gy"),
        to_prev(ylo, "gy"),
    )


def on_device(density, design_mask, velocity, adjoint_source, adjoint_start):
    depth, height, width = density.shape
    tables = cone_tables(height, width)
    blocks = depth // GROUP
    half = blocks // 2
    zlo = to_next(adjoint_start[:, depth - 1], "gz")
    zhi = to_prev(adjoint_start[:, 0], "gz")
    arrived = exchange(faces_of(adjoint_start))
    inner = sweep(
        adjoint_start, adjoint_source, density, arrived, 1, blocks - 2, faces=True
    )
    outer = sweep(
        adjoint_start, adjoint_source, density, arrived, 0, 2, blocks - 1,
        zlo=zlo, zhi=zhi, faces=True, held=inner[1:], onto=[(0, inner[0])],
    )
    once = outer[0]
    zlo = to_next(once[:, depth - 1], "gz")
    zhi = to_prev(once[:, 0], "gz")
    arrived = exchange(outer[1:])
    run = functools.partial(sweep, once, adjoint_source, density, arrived, velocity=velocity)
    inner = run(1, half - 1)
    adjoint, *low = run(0, 1, zlo=zlo, onto=list(enumerate(inner)))
    adjoint, *high = run(half, half, zhi=zhi, sens_base=half, onto=[(0, adjoint)])
    low = cone_filter(*low, tables)
    above = to_prev(low, "gz")
    high = cone_filter(*high, tables)
    below = to_next(high, "gz")
    moved = density_step(low, high, above, density, design_mask, 1)
    density_next = density_step(below, low, high, density, design_mask, 0, moved)
    return (density_next, adjoint)


def solution(mesh):
    return jax.shard_map(
        on_device,
        mesh=mesh,
        in_specs=(
            P("gz", "gy", "gx"),
            P("gz", "gy", "gx"),
            P(None, "gz", "gy", "gx"),
            P(None, "gz", "gy", "gx"),
            P(None, "gz", "gy", "gx"),
        ),
        out_specs=(P("gz", "gy", "gx"), P(None, "gz", "gy", "gx")),
        check_vma=False,
    )
```

```python
import functools
import math

import jax
import jax.numpy as jnp
import ml_dtypes
import numpy as np
from jax import lax
from jax.experimental import pallas as pl
from jax.experimental.pallas import tpu as pltpu
from jax.sharding import PartitionSpec as P

NX = 512
NY = 512
RADIUS = 32
RADIUS_Z = 16
OMEGA = 0.8
ALPHA_MAX = 12.0
MOVE_STEP = 8.0
GROUP = 4
LANES = 128
VMEM = 48 * 2**20


def params():
    return pltpu.CompilerParams(
        vmem_limit_bytes=VMEM, dimension_semantics=("arbitrary",)
    )


def cost(flops, size):
    return pl.CostEstimate(flops=int(flops), bytes_accessed=int(size), transcendentals=0)


def to_next(array, axis):
    count = lax.axis_size(axis)
    return lax.ppermute(array, axis, [(i, (i + 1) % count) for i in range(count)])


def to_prev(array, axis):
    count = lax.axis_size(axis)
    return lax.ppermute(array, axis, [((i + 1) % count, i) for i in range(count)])


def across_y(first_rows, last_rows):
    if lax.axis_size("gy") == 2:
        count = last_rows.shape[0]
        arrived = to_next(jnp.concatenate([last_rows, first_rows], axis=0), "gy")
        return arrived[:count], arrived[count:]
    return to_next(last_rows, "gy"), to_prev(first_rows, "gy")


def pack_faces(plane, lane, column, xlo, xhi, ylo, yhi):
    height = plane.shape[0]
    here = lane == column
    xlo[...] = jnp.where(here, pltpu.roll(plane, column, 1), xlo[...])
    xhi[...] = jnp.where(here, pltpu.roll(plane, column + 1, 1), xhi[...])
    ylo[pl.ds(column, 1), :] = plane[0:1]
    yhi[pl.ds(column, 1), :] = plane[height - 1 : height]


def faces_kernel(depth, adj, xlo, xhi, ylo, yhi):
    step = pl.program_id(0)

    @pl.when(step == 0)
    def _():
        for ref in (xlo, xhi, ylo, yhi):
            ref[...] = jnp.zeros_like(ref)

    lane = lax.broadcasted_iota(jnp.int32, xlo.shape, 1)
    for j in range(GROUP):
        for c in range(3):
            pack_faces(
                adj[c, j], lane, c * depth + step * GROUP + j, xlo, xhi, ylo, yhi
            )


def face_shapes(depth, height):
    return [jax.ShapeDtypeStruct((height, LANES), jnp.float32)] * 2 + [
        jax.ShapeDtypeStruct((3 * depth, LANES), jnp.float32)
    ] * 2


def whole_spec(shape):
    return pl.BlockSpec(shape, lambda i: (0,) * len(shape))


def faces_of(adjoint):
    _, depth, height, width = adjoint.shape
    shapes = face_shapes(depth, height)
    return pl.pallas_call(
        functools.partial(faces_kernel, depth),
        grid=(depth // GROUP,),
        in_specs=[pl.BlockSpec((3, GROUP, height, width), lambda i: (0, i, 0, 0))],
        out_specs=[whole_spec(s.shape) for s in shapes],
        out_shape=shapes,
        compiler_params=params(),
        cost_estimate=cost(10 * adjoint.size, 4 * adjoint.size),
        name="faces",
    )(adjoint)


def pack_edges(value, lane, j, pack_lo, pack_hi):
    turned = pltpu.roll(value, RADIUS * (j + 1) % LANES, 1)
    group = lane // RADIUS
    low = jnp.where(group == (j + 1) % GROUP, turned, 0.0)
    high = jnp.where(group == j, turned, 0.0)
    if j == 0:
        pack_lo[0] = low
        pack_hi[0] = high
    else:
        pack_lo[0] += low
        pack_hi[0] += high


def edges_kernel(cells, pack_lo, pack_hi):
    lane = lax.broadcasted_iota(jnp.int32, cells.shape[1:], 1)
    for j in range(GROUP):
        pack_edges(cells[j], lane, j, pack_lo, pack_hi)


def edges_of(cells):
    planes, height, width = cells.shape
    packed = pl.BlockSpec((1, height, LANES), lambda i: (i, 0, 0))
    return pl.pallas_call(
        edges_kernel,
        grid=(planes // GROUP,),
        in_specs=[pl.BlockSpec((GROUP, height, width), lambda i: (i, 0, 0))],
        out_specs=[packed] * 2,
        out_shape=[jax.ShapeDtypeStruct((planes // GROUP, height, LANES), jnp.float32)] * 2,
        compiler_params=params(),
        cost_estimate=cost(4 * cells.size, 6 * cells.size),
        name="edges",
    )(cells)


def sweep_kernel(conf, *refs):
    depth, first, stride, use_lo, use_hi, faces, fresh, sens = conf
    refs = list(refs)
    adj, prev, follow, source, density, xleft, xright, yabove, ybelow = refs[:9]
    refs = refs[9:]
    zlo = refs.pop(0) if use_lo else None
    zhi = refs.pop(0) if use_hi else None
    velocity = refs.pop(0) if sens else None
    if faces and not fresh:
        held = refs[:4]
        refs = refs[4:]
    aliased = conf.aliased
    refs = refs[aliased:]
    out = refs.pop(0)
    if faces:
        packs = refs[:4]
        refs = refs[4:]
    if sens:
        sens_out, pack_lo, pack_hi = refs
    step = pl.program_id(0)
    block = first + stride * step
    height, width = out.shape[2:]
    if faces:

        @pl.when(step == 0)
        def _():
            for at in range(4):
                if fresh:
                    packs[at][...] = jnp.zeros_like(packs[at])
                else:
                    packs[at][...] = held[at][...]

    lane = lax.broadcasted_iota(jnp.int32, (height, width), 1)
    row = lax.broadcasted_iota(jnp.int32, (height, width), 0)
    last_block = depth // GROUP - 1
    for j in range(GROUP):
        dens = density[j]
        weight = OMEGA * (1.0 + dens) / (18.0 - 6.0 * dens)
        total = None
        for c in range(3):
            column = c * depth + block * GROUP + j
            plane = adj[c, j]
            if j > 0:
                below = adj[c, j - 1]
            else:
                below = prev[c, 0]
                if use_lo:
                    below = jnp.where(block == 0, zlo[c], below)
            if j < GROUP - 1:
                above = adj[c, j + 1]
            else:
                above = follow[c, 0]
                if use_hi:
                    above = jnp.where(block == last_block, zhi[c], above)
            beside = above + below
            beside += jnp.where(
                row == 0, yabove[pl.ds(column, 1), :], pltpu.roll(plane, 1, 0)
            )
            beside += jnp.where(
                row == height - 1,
                ybelow[pl.ds(column, 1), :],
                pltpu.roll(plane, height - 1, 0),
            )
            beside += jnp.where(
                lane == 0,
                pltpu.roll(xleft[...], (LANES - column) % LANES, 1),
                pltpu.roll(plane, 1, 1),
            )
            beside += jnp.where(
                lane == width - 1,
                pltpu.roll(xright[...], LANES - 1 - column, 1),
                pltpu.roll(plane, width - 1, 1),
            )
            relaxed = (1.0 - OMEGA) * plane + weight * (
                source[c, j].astype(jnp.float32) + beside
            )
            out[c, j] = relaxed
            if faces:
                pack_faces(relaxed, lane, column, *packs)
            if sens:
                part = velocity[c, j].astype(jnp.float32) * relaxed
                total = part if total is None else total + part
        if sens:
            near = 1.0 / (1.0 + dens)
            value = (-2.0 * ALPHA_MAX) * near * near * total
            sens_out[j] = value
            pack_edges(value, lane, j, pack_lo, pack_hi)


class Conf(tuple):
    aliased = 0


def sweep(
    adjoint,
    source,
    density,
    arrived,
    first,
    count,
    stride=1,
    zlo=None,
    zhi=None,
    faces=False,
    held=None,
    velocity=None,
    sens_base=0,
    onto=(),
):
    _, depth, height, width = adjoint.shape
    sens = velocity is not None
    conf = Conf(
        (depth, first, stride, zlo is not None, zhi is not None, faces, held is None, sens)
    )
    conf.aliased = len(onto)

    def at(i):
        return first + stride * i

    block = pl.BlockSpec((3, GROUP, height, width), lambda i: (0, at(i), 0, 0))
    plane_shape = (3, 1, height, width)
    operands = [adjoint, adjoint, adjoint, source, density, *arrived]
    in_specs = [
        block,
        pl.BlockSpec(plane_shape, lambda i: (0, jnp.maximum(at(i) * GROUP - 1, 0), 0, 0)),
        pl.BlockSpec(
            plane_shape, lambda i: (0, jnp.minimum(at(i) * GROUP + GROUP, depth - 1), 0, 0)
        ),
        block,
        pl.BlockSpec((GROUP, height, width), lambda i: (at(i), 0, 0)),
    ]
    in_specs += [whole_spec(a.shape) for a in arrived]
    for face in (zlo, zhi):
        if face is not None:
            operands.append(face)
            in_specs.append(whole_spec(face.shape))
    if sens:
        operands.append(velocity)
        in_specs.append(block)
    if held is not None:
        operands += list(held)
        in_specs += [whole_spec(a.shape) for a in held]
    aliases = {}
    for index, array in onto:
        aliases[len(operands)] = index
        operands.append(array)
        in_specs.append(pl.BlockSpec(memory_space=pl.ANY))
    out_specs = [block]
    out_shape = [jax.ShapeDtypeStruct(adjoint.shape, jnp.float32)]
    if faces:
        shapes = face_shapes(depth, height)
        out_shape += shapes
        out_specs += [whole_spec(s.shape) for s in shapes]
    if sens:
        half = depth // 2
        out_shape += [jax.ShapeDtypeStruct((half, height, width), jnp.float32)] + [
            jax.ShapeDtypeStruct((half // GROUP, height, LANES), jnp.float32)
        ] * 2
        out_specs += [
            pl.BlockSpec((GROUP, height, width), lambda i: (at(i) - sens_base, 0, 0))
        ] + [pl.BlockSpec((1, height, LANES), lambda i: (at(i) - sens_base, 0, 0))] * 2
    cells = 3 * GROUP * count * height * width
    return pl.pallas_call(
        functools.partial(sweep_kernel, conf),
        grid=(count,),
        in_specs=in_specs,
        out_specs=out_specs,
        out_shape=out_shape,
        input_output_aliases=aliases,
        compiler_params=params(),
        cost_estimate=cost(40 * cells, 14 * cells),
        name="sweep",
    )(*operands)


def parts_of(table, axis):
    high = table.astype(ml_dtypes.bfloat16)
    low = (table - high.astype(np.float64)).astype(ml_dtypes.bfloat16)
    return jnp.asarray(np.concatenate([high, high, low], axis=axis))


def real_dft(length):
    half = length // 2
    waves = np.concatenate([np.arange(half + 1), np.arange(1, half)])
    phase = 2.0 * math.pi / length * (waves[:, None] * np.arange(length)[None, :] % length)
    table = np.where(np.arange(length)[:, None] <= half, np.cos(phase), np.sin(phase))
    scale = np.full((length, 1), math.sqrt(2.0 / length))
    scale[0] = scale[half] = math.sqrt(1.0 / length)
    return table * scale, waves


def cone_tables(height, width):
    long_x = -(-(width + 2 * RADIUS) // LANES) * LANES
    long_y = height + 2 * RADIUS
    basis_x, waves_x = real_dft(long_x)
    basis_y, waves_y = real_dft(long_y)
    reach = np.arange(-RADIUS, RADIUS + 1)
    cone = np.maximum(0.0, RADIUS - np.sqrt(reach[:, None] ** 2.0 + reach[None, :] ** 2.0))
    cone = cone / np.sum(cone)
    cos_y = np.cos(2.0 * math.pi / long_y * waves_y[:, None] * reach[None, :])
    cos_x = np.cos(2.0 * math.pi / long_x * waves_x[:, None] * reach[None, :])
    spectrum = (cos_y @ cone @ cos_x.T).astype(np.float32)
    into_x = np.zeros((GROUP, width + LANES, long_x))
    for j in range(GROUP):
        into_x[j, :width] = basis_x[:, RADIUS : RADIUS + width].T
        left = width + RADIUS * j
        into_x[j, left : left + RADIUS] = basis_x[:, :RADIUS].T
        right = width + RADIUS * ((j + 1) % GROUP)
        into_x[j, right : right + RADIUS] = basis_x[:, RADIUS + width : 2 * RADIUS + width].T
    tables = [
        parts_of(into_x, 1),
        parts_of(basis_y, 1),
        parts_of(basis_y[:, RADIUS : RADIUS + height].T, 1),
        parts_of(basis_x[:, RADIUS : RADIUS + width], 0),
        jnp.asarray(spectrum),
    ]
    return tables


def triple(value, axis):
    high = value.astype(jnp.bfloat16)
    low = (value - high.astype(jnp.float32)).astype(jnp.bfloat16)
    return jnp.concatenate([high, low, high], axis=axis)


dot = functools.partial(jnp.dot, preferred_element_type=jnp.float32)


def cone_kernel(
    own, left, right,
    above, above_left, above_right,
    below, below_left, below_right,
    into_x, into_y, from_y, from_x, spectrum, out,
):
    for j in range(GROUP):

        def wide(mid, lhs, rhs):
            group = lax.broadcasted_iota(jnp.int32, lhs.shape, 1) // RADIUS
            return jnp.concatenate([mid, jnp.where(group == j, lhs, rhs)], axis=1)

        cells = jnp.concatenate(
            [
                wide(above[j], above_left[0], above_right[0]),
                wide(own[j], left[0], right[0]),
                wide(below[j], below_left[0], below_right[0]),
            ],
            axis=0,
        )
        waves = dot(triple(cells, 1), into_x[j])
        waves = dot(into_y[...], triple(waves, 0)) * spectrum[...]
        rows = dot(from_y[...], triple(waves, 0))
        out[j] = dot(triple(rows, 1), from_x[...])


def cone_filter(sens, pack_lo, pack_hi, tables, parts=1):
    planes, height, width = sens.shape
    steps = planes // GROUP
    left = to_next(pack_hi, "gx")
    right = to_prev(pack_lo, "gx")
    above, below = across_y(sens[:, :RADIUS], sens[:, height - RADIUS :])
    sides = jnp.concatenate([left[:, :RADIUS], right[:, :RADIUS]], axis=0)
    far_sides = jnp.concatenate(
        [left[:, height - RADIUS :], right[:, height - RADIUS :]], axis=0
    )
    above_sides, below_sides = across_y(sides, far_sides)
    each = steps // parts
    long_y = height + 2 * RADIUS

    def part(base):
        packed = pl.BlockSpec((1, height, LANES), lambda i: (base + i, 0, 0))
        strip_specs = [
            pl.BlockSpec((GROUP, RADIUS, width), lambda i: (base + i, 0, 0)),
            pl.BlockSpec((1, RADIUS, LANES), lambda i: (base + i, 0, 0)),
            pl.BlockSpec((1, RADIUS, LANES), lambda i: (steps + base + i, 0, 0)),
        ]
        block = pl.BlockSpec((GROUP, height, width), lambda i: (base + i, 0, 0))
        return pl.pallas_call(
            cone_kernel,
            grid=(each,),
            in_specs=[block, packed, packed]
            + strip_specs * 2
            + [whole_spec(t.shape) for t in tables],
            out_specs=pl.BlockSpec((GROUP, height, width), lambda i: (i, 0, 0)),
            out_shape=jax.ShapeDtypeStruct((each * GROUP, height, width), jnp.float32),
            compiler_params=params(),
            cost_estimate=cost(
                each * GROUP * 24 * long_y * 256 * (long_y + 256), 16 * sens.size // parts
            ),
            name="cone",
        )(
            sens, left, right,
            above, above_sides, above_sides, below, below_sides, below_sides,
            *tables,
        )

    return [part(at * each) for at in range(parts)]


def step_kernel(count, *refs):
    density, mask, out = refs[count], refs[count + 1], refs[-1]
    cells = [(part, z) for part in refs[:count] for z in range(part.shape[0])]
    planes, rows = out.shape[:2]
    length = RADIUS_Z + 1
    for start in range(0, rows, 8):
        at = slice(start, start + 8)

        def cell(z):
            part, own = cells[z]
            return part[own, at]

        box = cell(0)
        for z in range(1, length):
            box = box + cell(z)
        boxes = [box]
        for z in range(1, 2 * planes):
            box = box + (cell(z + length - 1) - cell(z - 1))
            boxes.append(box)
        tent = boxes[0]
        for z in range(1, length):
            tent = tent + boxes[z]
        for z in range(planes):
            if z > 0:
                tent = tent + (boxes[z + length - 1] - boxes[z - 1])
            moved = density[z, at] - (MOVE_STEP / float(length * length)) * tent
            moved = jnp.minimum(jnp.maximum(moved, 0.0), 1.0)
            out[z, at] = jnp.where(mask[z, at] == 1, 0.0, moved)


def density_step(parts, density, mask, half, onto=None):
    depth, height, width = density.shape
    planes = depth // 2
    size = planes * height * width
    rows = 32
    blocks = [pl.BlockSpec((p.shape[0], rows, width), lambda i: (0, i, 0)) for p in parts]
    placed = pl.BlockSpec((planes, rows, width), lambda i: (half, i, 0))
    operands = [*parts, density, mask]
    in_specs = blocks + [placed] * 2
    aliases = {}
    if onto is not None:
        aliases[len(operands)] = 0
        operands.append(onto)
        in_specs.append(pl.BlockSpec(memory_space=pl.ANY))
    return pl.pallas_call(
        functools.partial(step_kernel, len(parts)),
        grid=(height // rows,),
        in_specs=in_specs,
        out_specs=placed,
        out_shape=jax.ShapeDtypeStruct(density.shape, jnp.float32),
        input_output_aliases=aliases,
        compiler_params=params(),
        cost_estimate=cost(12 * size, 24 * size),
        name="step",
    )(*operands)


def exchange(faces):
    xlo, xhi, ylo, yhi = faces
    return (
        to_next(xhi, "gx"),
        to_prev(xlo, "gx"),
        *across_y(ylo, yhi),
    )


def on_device(density, design_mask, velocity, adjoint_source, adjoint_start):
    depth, height, width = density.shape
    tables = cone_tables(height, width)
    blocks = depth // GROUP
    half = blocks // 2
    zlo = to_next(adjoint_start[:, depth - 1], "gz")
    zhi = to_prev(adjoint_start[:, 0], "gz")
    arrived = exchange(faces_of(adjoint_start))
    inner = sweep(
        adjoint_start, adjoint_source, density, arrived, 1, blocks - 2, faces=True
    )
    outer = sweep(
        adjoint_start, adjoint_source, density, arrived, 0, 2, blocks - 1,
        zlo=zlo, zhi=zhi, faces=True, held=inner[1:], onto=[(0, inner[0])],
    )
    once = outer[0]
    zlo = to_next(once[:, depth - 1], "gz")
    zhi = to_prev(once[:, 0], "gz")
    arrived = exchange(outer[1:])
    run = functools.partial(sweep, once, adjoint_source, density, arrived, velocity=velocity)
    inner = run(1, half - 1)
    adjoint, *low = run(0, 1, zlo=zlo, onto=list(enumerate(inner)))
    adjoint, *high = run(half, half, zhi=zhi, sens_base=half, onto=[(0, adjoint)])
    rim = to_prev(low[0], "gz")
    low = cone_filter(*low, tables)
    high = cone_filter(*high, tables, parts=2)
    below = [to_next(part, "gz") for part in high]
    above = cone_filter(rim, *edges_of(rim), tables)
    moved = density_step([*low, *high, *above], density, design_mask, 1)
    density_next = density_step([*below, *low, *high], density, design_mask, 0, moved)
    return (density_next, adjoint)


def solution(mesh):
    return jax.shard_map(
        on_device,
        mesh=mesh,
        in_specs=(
            P("gz", "gy", "gx"),
            P("gz", "gy", "gx"),
            P(None, "gz", "gy", "gx"),
            P(None, "gz", "gy", "gx"),
            P(None, "gz", "gy", "gx"),
        ),
        out_specs=(P("gz", "gy", "gx"), P(None, "gz", "gy", "gx")),
        check_vma=False,
    )
```
